256 devices in a mesh: row: 16 (over z, y_lo), col: 16 (over x, y_hi, core).
Axes of the slice: x: 4, y: 4 (y_hi: 2, y_lo: 2; y = y_hi * 2 + y_lo), z: 8, core: 2. Of those that a mesh axis runs over, the one named last changes fastest.
Arguments:
- tokens: bfloat16 [1024, 12288], P('col', 'row'), may hold values from -6 to 6
- in_weight: bfloat16 [12288, 24576], P('row', 'col'), may hold values from -0.0546875 to 0.0546875
- out_weight: bfloat16 [24576, 12288], P('col', 'row'), may hold values from -0.0390625 to 0.0390625
- out_grad: bfloat16 [1024, 12288], P('col', 'row'), may hold values from -6 to 6
Outputs:
- layer_out: bfloat16 [1024, 12288], P('col', 'row')
- token_grad: bfloat16 [1024, 12288], P('col', 'row')
- first_grad: bfloat16 [12288, 24576], P('row', 'col')
- second_grad: bfloat16 [24576, 12288], P('col', 'row')
The draws below stay inside these ranges and needn't reach their ends.
All inputs are finite; a program needn't handle non-finite values.
Results may differ from the reference program's by a relative error of at most 0.005.
Values may be sent and summed in bfloat16 or wider, within the bound.
No kernel may reach another device: no remote copies, remote signals or barrier semaphores. Data moves between devices by JAX's collectives and lax.ppermute only.
A program may use at most 128 MiB of HBM per device.

```python
import jax
import jax.numpy as jnp
from jax import lax

D = 12288
FF = 24576
TOKENS = 1024


def steps_of(rng, extent, pieces, low, largest):
    gain = 1.0
    for dim, parts in pieces:
        heights = jax.random.uniform(jax.random.fold_in(jax.random.fold_in(rng, 6), dim), (parts,), jnp.float32, low / len(pieces), largest / len(pieces))
        gain = gain * jnp.repeat(jnp.exp(heights), extent[dim] // parts).reshape((-1,) + (1,) * (len(extent) - 1 - dim))
    return gain


def gaussian(rng, shape, spread, bound, cuts=(), kind=jnp.bfloat16):
    values = spread * jax.random.normal(rng, shape, jnp.float32)
    if cuts:
        values = values * steps_of(rng, shape, cuts, -0.22, 0.18)
    return jnp.clip(values, -bound, bound).astype(kind)


def setup_inputs(seed: int = 0) -> dict:
    arg_keys = jax.random.split(jax.random.key(seed), 5)
    tokens = gaussian(arg_keys[0], (TOKENS, D), 1.0, 6.0, ((0, 16), (1, 16)))
    in_weight = gaussian(arg_keys[1], (D, FF), D ** -0.5, 0.0546875, ((0, 16), (1, 16)))
    out_weight = gaussian(arg_keys[2], (FF, D), FF ** -0.5, 0.0390625, ((0, 16), (1, 16)))
    out_grad = gaussian(arg_keys[3], (TOKENS, D), 1.0, 6.0, ((0, 16), (1, 16)))
    return dict(tokens=tokens, in_weight=in_weight, out_weight=out_weight, out_grad=out_grad)


gelu_c = 0.7978845608
gelu_k = 0.044715


def gelu_value(pre):
    inner = jnp.tanh(gelu_c * (pre + gelu_k * pre * pre * pre))
    return 0.5 * pre * (1.0 + inner)


def gelu_slope(pre):
    inner = jnp.tanh(gelu_c * (pre + gelu_k * pre * pre * pre))
    return 0.5 * (1.0 + inner) + 0.5 * pre * (1.0 - inner * inner) * gelu_c * (1.0 + 3.0 * gelu_k * pre * pre)


def reference(tokens, in_weight, out_weight, out_grad):
    pre = jnp.dot(tokens, in_weight, preferred_element_type=jnp.float32)
    hidden = gelu_value(pre).astype(jnp.bfloat16)
    layer_out = jnp.dot(hidden, out_weight, preferred_element_type=jnp.float32).astype(jnp.bfloat16)
    hidden_grad = lax.dot_general(out_grad, out_weight, (((1,), (1,)), ((), ())), preferred_element_type=jnp.float32)
    pre_grad = (hidden_grad * gelu_slope(pre)).astype(jnp.bfloat16)
    first_grad = lax.dot_general(tokens, pre_grad, (((0,), (0,)), ((), ())), preferred_element_type=jnp.float32).astype(jnp.bfloat16)
    second_grad = lax.dot_general(hidden, out_grad, (((0,), (0,)), ((), ())), preferred_element_type=jnp.float32).astype(jnp.bfloat16)
    token_grad = lax.dot_general(pre_grad, in_weight, (((1,), (1,)), ((), ())), preferred_element_type=jnp.float32).astype(jnp.bfloat16)
    return layer_out, token_grad, first_grad, second_grad
```

```python
import jax
import jax.numpy as jnp
from jax import lax
from jax.experimental import pallas as pl
from jax.experimental.pallas import tpu as pltpu
from jax.sharding import Mesh, PartitionSpec as P

gelu_c = 0.7978845608
gelu_k = 0.044715
bf16 = jnp.bfloat16
f32 = jnp.float32

NZ, NX = 8, 4


def gelu_value(pre):
    inner = jnp.tanh(gelu_c * (pre + gelu_k * pre * pre * pre))
    return 0.5 * pre * (1.0 + inner)


def gelu_slope(pre):
    inner = jnp.tanh(gelu_c * (pre + gelu_k * pre * pre * pre))
    return 0.5 * (1.0 + inner) + 0.5 * pre * (1.0 - inner * inner) * gelu_c * (
        1.0 + 3.0 * gelu_k * pre * pre
    )


def dot_plain(left, right):
    return jnp.dot(left, right, preferred_element_type=f32)


def dot_last(left, right):
    return lax.dot_general(left, right, (((1,), (1,)), ((), ())), preferred_element_type=f32)


def dot_first(left, right):
    return lax.dot_general(left, right, (((0,), (0,)), ((), ())), preferred_element_type=f32)


def shift(a, axis, k):
    n = lax.axis_size(axis)
    return lax.ppermute(a, axis, [(i, (i + k) % n) for i in range(n)])


def place_kernel(slots, mine, theirs, out, sems):
    copies = []
    for i in range(16):
        src = mine if i < 8 else theirs
        copies.append(pltpu.make_async_copy(src.at[i % 8], out.at[slots[i]], sems.at[i]))
    for c in copies:
        c.start()
    for c in copies:
        c.wait()


def place(mine, theirs, slots):
    return pl.pallas_call(
        place_kernel,
        out_shape=jax.ShapeDtypeStruct((16,) + mine.shape[1:], mine.dtype),
        in_specs=[
            pl.BlockSpec(memory_space=pltpu.SMEM),
            pl.BlockSpec(memory_space=pl.ANY),
            pl.BlockSpec(memory_space=pl.ANY),
        ],
        out_specs=pl.BlockSpec(memory_space=pl.ANY),
        scratch_shapes=[pltpu.SemaphoreType.DMA((16,))],
        cost_estimate=pl.CostEstimate(flops=0, bytes_accessed=4 * mine.size * 2, transcendentals=0),
    )(slots, mine, theirs)


def gather_col(t, slots):
    n, d = t.shape
    pair = jnp.stack([t, shift(t, "yh", 1)])
    back = [shift(pair, "x", k) for k in (3, 2, 1)]
    mine = jnp.concatenate([pair] + back)
    theirs = shift(mine, "c", 1)
    return place(mine, theirs, slots).reshape(NZ, 2, n, d)


def sum_z(term, first_up):
    up_ks = (4, 3, 2, 1) if first_up else (3, 2, 1)
    down_ks = (5, 6, 7) if first_up else (4, 5, 6, 7)
    up = down = None
    order = []
    for i in range(4):
        if i < len(up_ks):
            order.append(("up", up_ks[i]))
        if i < len(down_ks):
            order.append(("down", down_ks[i]))
    for way, k in order:
        if way == "up":
            v = term(k) if up is None else term(k) + up.astype(f32)
            up = shift(v.astype(bf16), "z", 1)
        else:
            v = term(k) if down is None else term(k) + down.astype(f32)
            down = shift(v.astype(bf16), "z", -1)
    return term(0) + up.astype(f32) + down.astype(f32)


def ring_z(own, first_up):
    got = [own] + [None] * 7
    n_up = 4 if first_up else 3
    up = down = own
    for i in range(4):
        if i < n_up:
            up = shift(up, "z", 1)
            got[7 - i] = up
        if i < 7 - n_up:
            down = shift(down, "z", -1)
            got[1 + i] = down
    return got


def scatter_col(parts, keep_e, z):
    whole = jnp.stack(parts)
    send = lax.dynamic_index_in_dim(whole, 1 - keep_e, 1, keepdims=False)
    keep = lax.dynamic_index_in_dim(whole, keep_e, 1, keepdims=False)
    both = keep + shift(send, "c", 1)
    both = both.astype(bf16)
    turned = lax.dynamic_slice_in_dim(jnp.concatenate([both, both]), (NZ - z) % NZ, NZ, 0)
    got = lax.all_to_all(turned, ("x", "yh"), 0, 0, tiled=True)
    return jnp.sum(got.astype(f32), axis=0).astype(bf16)


def per_device(tokens, in_weight, out_weight, out_grad):
    z, yl = lax.axis_index("z"), lax.axis_index("yl")
    x, yh, c = lax.axis_index("x"), lax.axis_index("yh"), lax.axis_index("c")
    n, d = tokens.shape
    ff = in_weight.shape[1]
    i = jnp.arange(16, dtype=jnp.int32)
    rc, rx, ry = i // 8, (i % 8) // 2, i % 2
    owner_z = 2 * ((x + rx) % NX) + (yh ^ ry)
    slots = ((owner_z - z) % NZ) * 2 + (c ^ rc ^ yl)
    keep_e = yl ^ c

    tok = gather_col(tokens, slots)
    grad = gather_col(out_grad, slots)

    pre2 = sum_z(lambda k: dot_plain(tok[k].reshape(2 * n, d), in_weight), True)
    pre = pre2[:n] + shift(pre2[n:].astype(bf16), "yl", 1).astype(f32)

    from_y = {}
    for ks in ((4, 5), (3, 6), (2, 7), (1, 0)):
        block = jnp.concatenate([grad[k, 1] for k in ks])
        got = shift(dot_last(block, out_weight).astype(bf16), "yl", 1)
        for j, k in enumerate(ks):
            from_y[k] = got[j * n : (j + 1) * n]
    hid = sum_z(lambda k: dot_last(grad[k, 0], out_weight) + from_y[k].astype(f32), False)

    hidden = gelu_value(pre).astype(bf16)
    pre_grad = (hid * gelu_slope(pre)).astype(bf16)

    hids = ring_z(jnp.concatenate([hidden, shift(hidden, "yl", 1)]), True)
    layer_out = scatter_col([dot_plain(h, out_weight).reshape(2, n, d) for h in hids], keep_e, z)

    pgs = ring_z(pre_grad, False)
    pairs = [None] * NZ
    for ks in ((0,), (1, 7), (2, 6), (3, 5), (4,)):
        block = pgs[ks[0]] if len(ks) == 1 else jnp.concatenate([pgs[k] for k in ks])
        got = shift(block, "yl", 1)
        for j, k in enumerate(ks):
            pairs[k] = jnp.concatenate([pgs[k], got[j * n : (j + 1) * n]])
    token_grad = scatter_col([dot_last(p, in_weight).reshape(2, n, d) for p in pairs], keep_e, z)

    all_tok = tok.reshape(16 * n, d)
    all_grad = grad.reshape(16 * n, d)
    first_grad = dot_first(all_tok, jnp.concatenate(pairs)).astype(bf16)
    second_grad = dot_first(jnp.concatenate(hids), all_grad).astype(bf16)
    return (layer_out, token_grad, first_grad, second_grad)


def solution(mesh):
    fine = Mesh(mesh.devices.reshape(8, 2, 4, 2, 2), ("z", "yl", "x", "yh", "c"))
    row, col = ("z", "yl"), ("x", "yh", "c")
    return jax.shard_map(
        per_device,
        mesh=fine,
        in_specs=(P(col, row), P(row, col), P(col, row), P(col, row)),
        out_specs=(P(col, row), P(col, row), P(row, col), P(col, row)),
        check_vma=False,
    )
```

```python
import jax
import jax.numpy as jnp
from jax import lax
from jax.experimental import pallas as pl
from jax.experimental.pallas import tpu as pltpu
from jax.sharding import Mesh, PartitionSpec as P

gelu_c = 0.7978845608
gelu_k = 0.044715
bf16 = jnp.bfloat16
f32 = jnp.float32

NZ, NX = 8, 4


def gelu_value(pre):
    inner = jnp.tanh(gelu_c * (pre + gelu_k * pre * pre * pre))
    return 0.5 * pre * (1.0 + inner)


def gelu_slope(pre):
    inner = jnp.tanh(gelu_c * (pre + gelu_k * pre * pre * pre))
    return 0.5 * (1.0 + inner) + 0.5 * pre * (1.0 - inner * inner) * gelu_c * (
        1.0 + 3.0 * gelu_k * pre * pre
    )


def dot_plain(left, right):
    return jnp.dot(left, right, preferred_element_type=f32)


def dot_last(left, right):
    return lax.dot_general(left, right, (((1,), (1,)), ((), ())), preferred_element_type=f32)


def dot_first(left, right):
    return lax.dot_general(left, right, (((0,), (0,)), ((), ())), preferred_element_type=f32)


def shift(a, axis, k, name=None):
    n = lax.axis_size(axis)
    with jax.named_scope(name or "move_" + axis):
        return lax.ppermute(a, axis, [(i, (i + k) % n) for i in range(n)])


def place_kernel(groups, table, mine, theirs, *outs):
    def take(s):
        at = lax.rem(s, 8)
        return jnp.where(s < 8, mine[at], theirs[at])

    n = mine.shape[1]
    for out, group in zip(outs, groups):
        for j, i in enumerate(group):
            out[j * n : (j + 1) * n] = take(table[i])
    outs[-1][0] = theirs[...]
    outs[-1][1] = mine[...]


def place(mine, theirs, groups, table):
    _, n, d = mine.shape
    vmem, smem = pl.BlockSpec(memory_space=pltpu.VMEM), pl.BlockSpec(memory_space=pltpu.SMEM)
    out = pl.pallas_call(
        lambda *refs: place_kernel(groups, *refs),
        out_shape=[jax.ShapeDtypeStruct((len(g) * n, d), bf16) for g in groups]
        + [jax.ShapeDtypeStruct((2, 8, n, d), bf16)],
        in_specs=[smem, vmem, vmem],
        out_specs=[vmem] * (len(groups) + 1),
        cost_estimate=pl.CostEstimate(flops=0, bytes_accessed=12 * mine.size, transcendentals=0),
        compiler_params=pltpu.CompilerParams(vmem_limit_bytes=8 << 20),
    )(table, mine, theirs)
    return out[:-1], out[-1]


def after_kernel(a, *rest):
    pass


def after(a, *earlier):
    any_ = pl.BlockSpec(memory_space=pl.ANY)
    return pl.pallas_call(
        after_kernel,
        out_shape=jax.ShapeDtypeStruct(a.shape, a.dtype),
        in_specs=[any_] * (1 + len(earlier)),
        out_specs=any_,
        input_output_aliases={0: 0},
        cost_estimate=pl.CostEstimate(flops=1, bytes_accessed=1, transcendentals=0),
        compiler_params=pltpu.CompilerParams(vmem_limit_bytes=1 << 17),
    )(a, *earlier)


def gather_x(t, earlier=(), later=()):
    pair = jnp.stack([t, shift(t, "yh", 1)])
    if earlier:
        pair = after(pair, *earlier)
    back = [shift(pair, "x", k) for k in (3, 2, 1)]
    if later:
        back[0] = after(back[0], *later)
    return jnp.concatenate([pair] + back)


def ring_z(own, first_up, behind, name):
    got = [own] + [None] * 7
    n_up = 4 if first_up else 3
    up = down = own
    for i in range(4):
        if i < n_up:
            if i in behind:
                up = after(up, behind[i])
                got[8 - i if i else 0] = up
            up = shift(up, "z", 1, f"{name}{7 - i}")
            got[7 - i] = up
        if i < 7 - n_up:
            if i in behind:
                down = after(down, behind[i]) if i or n_up == 0 else got[0]
                got[i] = down
            down = shift(down, "z", -1, f"{name}{1 + i}")
            got[1 + i] = down
    return got


def product_kernel(last, groups, table, *refs):
    near, far, w = refs[:8], refs[8 : 8 + len(groups)], refs[8 + len(groups)]
    send, keep, whole = refs[9 + len(groups) :]
    n, ff = near[0].shape
    z, flip, x, yh = table[16], table[17], table[18], table[19]

    def at(k):
        m = lax.rem(z + k, NZ)
        return lax.rem(m // 2 - x + NX, NX) * 2 + jnp.abs(lax.rem(m, 2) - yh)

    for k in range(NZ):
        whole[1 - flip, at(k)] = near[k][...]
    for block, ks in zip(far, groups):
        for j, k in enumerate(ks):
            whole[flip, at(k)] = block[j * n : (j + 1) * n]
    dims = (((1,), (1 if last else 0,)), ((), ()))
    for i, out in enumerate((send, keep)):
        left = whole[i].reshape(NZ * n, ff)
        for j in range(0, out.shape[-1], 256):
            right = w[j : j + 256, :] if last else w[:, j : j + 256]
            p = lax.dot_general(left, right, dims, preferred_element_type=f32)
            out[:, :, j : j + 256] = p.reshape(NZ, n, 256)


def products(near, far, groups, w, last, table):
    n, ff = near[0].shape
    d = w.shape[0] if last else w.shape[1]
    vmem = pl.BlockSpec(memory_space=pltpu.VMEM)
    return pl.pallas_call(
        lambda *refs: product_kernel(last, groups, *refs),
        out_shape=[jax.ShapeDtypeStruct((NZ, n, d), f32)] * 2
        + [jax.ShapeDtypeStruct((2, NZ, n, ff), bf16)],
        in_specs=[pl.BlockSpec(memory_space=pltpu.SMEM)] + [vmem] * (9 + len(far)),
        out_specs=[vmem] * 3,
        cost_estimate=pl.CostEstimate(
            flops=4 * NZ * n * ff * d, bytes_accessed=12 << 20, transcendentals=0
        ),
        compiler_params=pltpu.CompilerParams(vmem_limit_bytes=15 << 20),
    )(table, *near, *far, w)


def scatter_x(keep, got, name):
    sent = [(keep[r] + got[r]).astype(bf16) for r in range(1, 8)]
    total = keep[0] + got[0]
    for r in range(1, 8):
        rx, ry = r // 2, r % 2
        pairs = [(i, (i // 2 + rx) % NX * 2 + (i % 2 ^ ry)) for i in range(8)]
        with jax.named_scope(f"{name}{r}"):
            total = total + lax.ppermute(sent[r - 1], ("x", "yh"), pairs).astype(f32)
    return sent, total.astype(bf16)


def per_device(tokens, in_weight, out_weight, out_grad):
    z, yl = lax.axis_index("z"), lax.axis_index("yl")
    x, yh, c = lax.axis_index("x"), lax.axis_index("yh"), lax.axis_index("c")
    n, d = tokens.shape
    ff = in_weight.shape[1]
    i = jnp.arange(16, dtype=jnp.int32)
    to_z, to_yl = (z + i // 2) % NZ, yl ^ (i % 2)
    src = (to_yl ^ c) * 8 + (to_z // 2 - x) % NX * 2 + (to_z % 2 ^ yh)
    table = jnp.concatenate([src, jnp.stack([z, yl ^ c, x, yh]).astype(src.dtype)])

    def up(a, name="pieces"):
        return shift(a, "z", 1, name + "_up")

    def down(a, name="pieces"):
        return shift(a, "z", -1, name + "_down")

    def plus(got, product):
        return (product + got.astype(f32)).astype(bf16)

    mine = gather_x(tokens)
    tok, all_tok = place(
        mine, shift(mine, "c", 1), [(2 * k, 2 * k + 1) for k in range(NZ)], table
    )

    def pre_term(k, *earlier):
        return dot_plain(after(tok[k], *earlier) if earlier else tok[k], in_weight)

    def hid_term(k, got, *earlier):
        block = after(grad[k], *earlier) if earlier else grad[k]
        return dot_last(block, out_weight) + got.astype(f32)

    p4 = pre_term(4).astype(bf16)
    p_up = up(p4, "p4")
    p5 = pre_term(5, p4).astype(bf16)
    p_down = down(p5, "p5")

    mine_g = gather_x(out_grad, [mine], [p5])
    theirs_g = shift(mine_g, "c", 1)

    p3 = plus(p_up, pre_term(3, p5))
    p_up = up(p3, "p3")
    p6 = plus(p_down, pre_term(6, p3))
    p_down = down(p6, "p6")

    rounds = ((4, 3), (5, 2), (6, 1), (7, 0))
    groups = [(2 * k,) for k in range(NZ)] + [tuple(2 * k + 1 for k in ks) for ks in rounds]
    grad, all_grad = place(mine_g, theirs_g, groups, after(table, p6))
    grad, blocks = grad[:NZ], grad[NZ:]

    def to_y(block, name):
        return shift(dot_last(block, out_weight).astype(bf16), "yl", 1, name)

    y0 = to_y(blocks[0], "first_y")
    y1 = to_y(blocks[1], "second_y")
    y2 = to_y(blocks[2], "third_y")
    from_y = {
        k: got[j * n : (j + 1) * n] for got, ks in zip((y0, y1, y2), rounds) for j, k in enumerate(ks)
    }

    p2 = plus(p_up, pre_term(2, grad[0]))
    p_up = up(p2, "p2")
    p7 = plus(p_down, pre_term(7, p2))
    p_down = down(p7, "p7")

    h4 = hid_term(4, from_y[4], p7).astype(bf16)
    h_down = down(h4, "h4")

    p1 = plus(p_up, pre_term(1, p7))
    p_up = up(p1, "p1")

    h3 = hid_term(3, from_y[3], p1, h4).astype(bf16)
    h_up = up(h3, "h3")

    pre2 = pre_term(0, h3) + p_up.astype(f32) + p_down.astype(f32)
    pre_far = pre2[n:].astype(bf16)
    pre_got = shift(pre_far, "yl", 1, "pre_y")
    y3 = to_y(after(blocks[3], pre_far), "fourth_y")
    from_y[7], from_y[0] = y3[:n], y3[n:]

    h5 = plus(h_down, hid_term(5, from_y[5], pre_far))
    h_down = down(h5, "h5")
    h2 = plus(h_up, hid_term(2, from_y[2], pre_far))
    h_up = up(h2, "h2")

    pre = pre2[:n] + pre_got.astype(f32)
    hidden = gelu_value(pre).astype(bf16)

    h6 = plus(h_down, hid_term(6, from_y[6], hidden))
    h_down = down(h6, "h6")
    h1 = plus(h_up, hid_term(1, from_y[1], hidden))
    h_up = up(h1, "h1")
    h7 = plus(h_down, hid_term(7, from_y[7]))
    h_down = down(h7, "h7")
    hid = hid_term(0, from_y[0]) + h_up.astype(f32) + h_down.astype(f32)
    pre_grad = (hid * gelu_slope(pre)).astype(bf16)

    hid0 = ring_z(hidden, True, {1: h1, 2: h7, 3: pre_grad}, "hidden_near")
    hid1 = ring_z(
        shift(hidden, "yl", 1, "hidden_y"), False, {0: h1, 1: h7, 2: pre_grad}, "hidden_far"
    )

    def to_pair(a, name, *earlier):
        return shift(after(a, *earlier) if earlier else a, "yl", 1, name)

    near = [pre_grad] + [None] * 7
    far0 = to_pair(pre_grad, "g0_y")
    near[7], near[1] = up(pre_grad, "g7"), down(pre_grad, "g1")
    far17 = to_pair(jnp.concatenate([near[1], near[7]]), "g17_y")
    near[6], near[2] = up(after(near[7], far0), "g6"), down(near[1], "g2")
    far26 = to_pair(jnp.concatenate([near[2], near[6]]), "g26_y")
    near[5], near[3] = up(near[6], "g5"), down(near[2], "g3")
    far35 = to_pair(jnp.concatenate([near[3], near[5]]), "g35_y")
    near[4] = up(after(near[5], far17), "g4")
    far4 = to_pair(near[4], "g4_y", far26)

    singles = [(k,) for k in range(NZ)]
    send, keep, all_hidden = products(
        hid0, hid1, singles, out_weight, False, after(table, near[3], near[5], far17, far26)
    )
    lo, layer_out = scatter_x(keep, shift(send, "c", 1, "out_core"), "out")

    groups = ((0,), (1, 7), (2, 6), (3, 5), (4,))
    far = [far0, far17, far26, far35, far4]
    send, keep, all_pre_grad = products(
        near, far, groups, in_weight, True, after(table, layer_out)
    )
    tg, token_grad = scatter_x(keep, shift(send, "c", 1, "token_core"), "token")

    def rows(a):
        return a.reshape(16 * n, a.shape[-1])

    second_grad = dot_first(rows(all_hidden), rows(all_grad)).astype(bf16)
    first_grad = dot_first(rows(after(all_tok, tg[-1])), rows(all_pre_grad)).astype(bf16)
    return (layer_out, token_grad, first_grad, second_grad)


def solution(mesh):
    fine = Mesh(mesh.devices.reshape(8, 2, 4, 2, 2), ("z", "yl", "x", "yh", "c"))
    row, col = ("z", "yl"), ("x", "yh", "c")
    return jax.shard_map(
        per_device,
        mesh=fine,
        in_specs=(P(col, row), P(row, col), P(col, row), P(col, row)),
        out_specs=(P(col, row), P(col, row), P(row, col), P(col, row)),
        check_vma=False,
    )
```

```python
import jax
import jax.numpy as jnp
from jax import lax
from jax.experimental import pallas as pl
from jax.experimental.pallas import tpu as pltpu
from jax.sharding import Mesh, PartitionSpec as P

gelu_c = 0.7978845608
gelu_k = 0.044715
bf16 = jnp.bfloat16
f32 = jnp.float32

NZ, NX = 8, 4


def gelu_value(pre):
    inner = jnp.tanh(gelu_c * (pre + gelu_k * pre * pre * pre))
    return 0.5 * pre * (1.0 + inner)


def gelu_slope(pre):
    inner = jnp.tanh(gelu_c * (pre + gelu_k * pre * pre * pre))
    return 0.5 * (1.0 + inner) + 0.5 * pre * (1.0 - inner * inner) * gelu_c * (
        1.0 + 3.0 * gelu_k * pre * pre
    )


def dot_plain(left, right):
    return jnp.dot(left, right, preferred_element_type=f32)


def dot_last(left, right):
    return lax.dot_general(left, right, (((1,), (1,)), ((), ())), preferred_element_type=f32)


def dot_first(left, right):
    return lax.dot_general(left, right, (((0,), (0,)), ((), ())), preferred_element_type=f32)


def shift(a, axis, k, name=None):
    n = lax.axis_size(axis)
    with jax.named_scope(name or "move_" + axis):
        return lax.ppermute(a, axis, [(i, (i + k) % n) for i in range(n)])


def place_kernel(groups, table, mine, theirs, *outs):
    def take(s):
        at = lax.rem(s, 8)
        return jnp.where(s < 8, mine[at], theirs[at])

    n = mine.shape[1]
    for out, group in zip(outs, groups):
        for j, i in enumerate(group):
            out[j * n : (j + 1) * n] = take(table[i])
    outs[-1][0] = theirs[...]
    outs[-1][1] = mine[...]


def place(mine, theirs, groups, table):
    _, n, d = mine.shape
    vmem, smem = pl.BlockSpec(memory_space=pltpu.VMEM), pl.BlockSpec(memory_space=pltpu.SMEM)
    out = pl.pallas_call(
        lambda *refs: place_kernel(groups, *refs),
        out_shape=[jax.ShapeDtypeStruct((len(g) * n, d), bf16) for g in groups]
        + [jax.ShapeDtypeStruct((2, 8, n, d), bf16)],
        in_specs=[smem, vmem, vmem],
        out_specs=[vmem] * (len(groups) + 1),
        cost_estimate=pl.CostEstimate(flops=0, bytes_accessed=12 * mine.size, transcendentals=0),
        compiler_params=pltpu.CompilerParams(vmem_limit_bytes=8 << 20),
    )(table, mine, theirs)
    return out[:-1], out[-1]


def after_kernel(a, *rest):
    pass


def after(a, *earlier):
    any_ = pl.BlockSpec(memory_space=pl.ANY)
    return pl.pallas_call(
        after_kernel,
        out_shape=jax.ShapeDtypeStruct(a.shape, a.dtype),
        in_specs=[any_] * (1 + len(earlier)),
        out_specs=any_,
        input_output_aliases={0: 0},
        cost_estimate=pl.CostEstimate(flops=1, bytes_accessed=1, transcendentals=0),
        compiler_params=pltpu.CompilerParams(vmem_limit_bytes=1 << 17),
    )(a, *earlier)


def gather_x(pair, earlier=(), later=()):
    if earlier:
        pair = after(pair, *earlier)
    back = [shift(pair, "x", k) for k in (3, 2, 1)]
    if later:
        back[0] = after(back[0], *later)
    return jnp.concatenate([pair] + back)


def ring_z(own, first_up, name):
    got = [own] + [None] * 7
    n_up = 4 if first_up else 3
    for i in range(4):
        if i < n_up:
            got[7 - i] = shift(got[(8 - i) % 8], "z", 1, f"{name}{7 - i}")
        if i < 7 - n_up:
            got[1 + i] = shift(got[i], "z", -1, f"{name}{1 + i}")
    return got


def product_kernel(last, layout, table, *refs):
    blocks, w = refs[: len(layout)], refs[len(layout)]
    send, keep, whole = refs[1 + len(layout) :]
    _, _, n, ff = whole.shape
    z, flip, x, yh = table[16], table[17], table[18], table[19]
    for block, parts in zip(blocks, layout):
        for j, (far, k) in enumerate(parts):
            m = lax.rem(z + k, NZ)
            to = lax.rem(m // 2 - x + NX, NX) * 2 + jnp.abs(lax.rem(m, 2) - yh)
            whole[flip if far else 1 - flip, to] = block[j * n : (j + 1) * n]
    dims = (((1,), (1 if last else 0,)), ((), ()))

    @pl.loop(0, send.shape[-1] // 256)
    def _(j):
        at = pl.ds(pl.multiple_of(j * 256, 256), 256)
        right = w[at, :] if last else w[:, at]
        for i, out in enumerate((send, keep)):
            left = whole[i].reshape(NZ * n, ff)
            p = lax.dot_general(left, right, dims, preferred_element_type=f32)
            out[:, :, at] = p.reshape(NZ, n, 256)


def products(n, blocks, layout, w, last, table):
    ff = blocks[0].shape[1]
    d = w.shape[0] if last else w.shape[1]
    vmem = pl.BlockSpec(memory_space=pltpu.VMEM)
    return pl.pallas_call(
        lambda *refs: product_kernel(last, layout, *refs),
        out_shape=[jax.ShapeDtypeStruct((NZ, n, d), f32)] * 2
        + [jax.ShapeDtypeStruct((2, NZ, n, ff), bf16)],
        in_specs=[pl.BlockSpec(memory_space=pltpu.SMEM)] + [vmem] * (len(blocks) + 1),
        out_specs=[vmem] * 3,
        cost_estimate=pl.CostEstimate(
            flops=4 * NZ * n * ff * d, bytes_accessed=12 << 20, transcendentals=0
        ),
        compiler_params=pltpu.CompilerParams(vmem_limit_bytes=15 << 20),
    )(table, *blocks, w)


def send_x(keep, got, name):
    total, sent, back = keep[:2] + got[:2], [], []
    for rx in range(1, NX):
        sent.append((keep[2 * rx : 2 * rx + 2] + got[2 * rx : 2 * rx + 2]).astype(bf16))
        back.append(shift(sent[-1], "x", rx, f"{name}_x{rx}"))

    def sums(*earlier):
        first = after(back[0], *earlier) if earlier else back[0]
        return total + sum(b.astype(f32) for b in [first] + back[1:])

    return sent, sums


def step_kernel(last, starts, splits, a, w, *refs):
    got, outs = refs[: len(starts)], refs[len(refs) - len(splits) :]
    rows = a.shape[0]
    dims = (((1,), (1 if last else 0,)), ((), ()))

    @pl.loop(0, outs[0].shape[1] // 256)
    def _(j):
        at = pl.ds(pl.multiple_of(j * 256, 256), 256)
        right = w[at, :] if last else w[:, at]
        p = lax.dot_general(a[...], right, dims, preferred_element_type=f32)
        for g, start in zip(got, starts):
            p = p + g[start : start + rows, at].astype(f32)
        for out, (first, end) in zip(outs, splits):
            out[:, at] = p[first:end].astype(out.dtype)


def step(a, w, last, got=(), outs=None, behind=()):
    rows, width = a.shape[0], w.shape[0] if last else w.shape[1]
    outs = outs or [(bf16, 0, rows)]
    vmem, any_ = pl.BlockSpec(memory_space=pltpu.VMEM), pl.BlockSpec(memory_space=pl.ANY)
    starts, splits = [g[1] for g in got], [o[1:] for o in outs]
    result = pl.pallas_call(
        lambda *refs: step_kernel(last, starts, splits, *refs),
        out_shape=[jax.ShapeDtypeStruct((end - first, width), t) for t, first, end in outs],
        in_specs=[vmem] * (2 + len(got)) + [any_] * len(behind),
        out_specs=[vmem] * len(outs),
        cost_estimate=pl.CostEstimate(
            flops=2 * rows * w.size, bytes_accessed=4 * rows * width, transcendentals=0
        ),
        compiler_params=pltpu.CompilerParams(vmem_limit_bytes=6 << 20),
    )(a, w, *[g[0] for g in got], *behind)
    return result if len(outs) > 1 else result[0]


def per_device(tokens, in_weight, out_weight, out_grad):
    z, yl = lax.axis_index("z"), lax.axis_index("yl")
    x, yh, c = lax.axis_index("x"), lax.axis_index("yh"), lax.axis_index("c")
    n, d = tokens.shape
    ff = in_weight.shape[1]
    i = jnp.arange(16, dtype=jnp.int32)
    to_z, to_yl = (z + i // 2) % NZ, yl ^ (i % 2)
    src = (to_yl ^ c) * 8 + (to_z // 2 - x) % NX * 2 + (to_z % 2 ^ yh)
    table = jnp.concatenate([src, jnp.stack([z, yl ^ c, x, yh]).astype(src.dtype)])

    def up(a, name="pieces"):
        return shift(a, "z", 1, name + "_up")

    def down(a, name="pieces"):
        return shift(a, "z", -1, name + "_down")

    def rows(a):
        return a.reshape(16 * n, a.shape[-1])

    other = shift(jnp.stack([tokens, out_grad]), "yh", 1, "both_yh")
    mine = gather_x(jnp.stack([tokens, other[0]]))
    pair_g = jnp.stack([out_grad, other[1]])
    tok, all_tok = place(
        mine, shift(mine, "c", 1), [(2 * k, 2 * k + 1) for k in range(NZ)], table
    )

    last_step = [mine]

    def chained(*given, **named):
        out = step(*given, behind=last_step[:], **named)
        last_step[:] = [out[0] if isinstance(out, (list, tuple)) else out]
        return out

    def pre_step(k, *got, **named):
        return chained(tok[k], in_weight, False, [(g, 0) for g in got], **named)

    def hid_step(k, *got, **named):
        return chained(grad[k], out_weight, True, [(g, 0) for g in got] + [from_y[k]], **named)

    def to_y(j, name):
        sent = chained(blocks[j], out_weight, True)
        got = shift(sent, "yl", 1, name)
        for i, k in enumerate(rounds[j]):
            from_y[k] = (got, i * n)

    from_y = {}
    rounds = ((4, 3), (5, 2), (6, 1), (7, 0))
    groups = [(2 * k,) for k in range(NZ)] + [tuple(2 * k + 1 for k in ks) for ks in rounds]

    p4 = pre_step(4)
    p_up = up(p4, "p4")
    p5 = pre_step(5)
    p_down = down(p5, "p5")
    p3 = pre_step(3, p_up)
    p_up = up(p3, "p3")
    p6 = pre_step(6, p_down)
    p_down = down(p6, "p6")

    mine_g = gather_x(pair_g, [mine], [p6])
    grad, all_grad = place(mine_g, shift(mine_g, "c", 1), groups, table)
    grad, blocks = grad[:NZ], grad[NZ:]

    to_y(0, "first_y")
    to_y(1, "second_y")
    p2 = pre_step(2, p_up)
    p_up = up(p2, "p2")
    p7 = pre_step(7, p_down)
    p_down = down(p7, "p7")
    p1 = pre_step(1, p_up)
    p_up = up(p1, "p1")
    h4 = hid_step(4)
    h_down = down(h4, "h4")
    to_y(2, "third_y")
    h3 = hid_step(3)
    h_up = up(h3, "h3")
    h5 = hid_step(5, h_down)
    h_down = down(h5, "h5")

    pre_near, pre_far = pre_step(0, p_up, p_down, outs=[(f32, 0, n), (bf16, n, 2 * n)])
    pre_got = shift(pre_far, "yl", 1, "pre_y")
    h2 = hid_step(2, h_up)
    h_up = up(h2, "h2")
    h6 = hid_step(6, h_down)
    h_down = down(h6, "h6")

    pre = pre_near + after(pre_got, h6).astype(f32)
    hidden = gelu_value(pre).astype(bf16)
    hidden_got = shift(hidden, "yl", 1, "hidden_y")
    last_step[:] = [hidden]
    to_y(3, "fourth_y")
    h1 = hid_step(1, h_up)
    h_up = up(h1, "h1")

    hid = ring_z(jnp.concatenate([hidden, hidden_got]), True, "hidden")

    h7 = hid_step(7, h_down)
    h_down = down(h7, "h7")
    last_step[:] = [hid[7], hid[1]]
    grad_sum = hid_step(0, h_up, h_down, outs=[(f32, 0, n)])
    pre_grad = (grad_sum * gelu_slope(pre)).astype(bf16)

    def to_pair(a, name, *earlier):
        return shift(after(a, *earlier) if earlier else a, "yl", 1, name)

    near = [pre_grad] + [None] * 7
    far0 = to_pair(pre_grad, "g0_y")
    near[7], near[1] = up(pre_grad, "g7"), down(pre_grad, "g1")
    far17 = to_pair(jnp.concatenate([near[1], near[7]]), "g17_y")
    near[6], near[2] = up(after(near[7], far0), "g6"), down(near[1], "g2")
    far26 = to_pair(jnp.concatenate([near[2], near[6]]), "g26_y")
    near[5], near[3] = up(after(near[6], far17), "g5"), down(near[2], "g3")
    far35 = to_pair(jnp.concatenate([near[3], near[5]]), "g35_y")
    near[4] = up(after(near[5], far26), "g4")
    far4 = to_pair(near[4], "g4_y")

    pairs = [((0, k), (1, k)) for k in range(NZ)]
    send, keep, all_hidden = products(
        n, hid, pairs, out_weight, False, after(table, far35, near[4])
    )
    out_sent, out_sums = send_x(keep, shift(send, "c", 1, "out_core"), "out")

    layout = [((0, k),) for k in range(NZ)]
    layout += [tuple((1, k) for k in ks) for ks in ((0,), (1, 7), (2, 6), (3, 5), (4,))]
    send, keep, all_pre_grad = products(
        n, near + [far0, far17, far26, far35, far4], layout, in_weight, True, after(table, *out_sent)
    )
    first_grad = dot_first(rows(all_tok), rows(all_pre_grad)).astype(bf16)
    total = out_sums()
    out_got = shift(total[1].astype(bf16), "yh", 1, "out_yh")
    layer_out = (total[0] + out_got.astype(f32)).astype(bf16)

    got = after(shift(send, "c", 1, "token_core"), first_grad, total)
    sent, sums = send_x(keep, got, "token")
    second_grad = dot_first(rows(all_hidden), rows(after(all_grad, *sent))).astype(bf16)
    total = sums(second_grad)
    got = shift(total[1].astype(bf16), "yh", 1, "token_yh")
    token_grad = (total[0] + got.astype(f32)).astype(bf16)
    return (layer_out, token_grad, first_grad, second_grad)


def solution(mesh):
    fine = Mesh(mesh.devices.reshape(8, 2, 4, 2, 2), ("z", "yl", "x", "yh", "c"))
    row, col = ("z", "yl"), ("x", "yh", "c")
    return jax.shard_map(
        per_device,
        mesh=fine,
        in_specs=(P(col, row), P(row, col), P(col, row), P(col, row)),
        out_specs=(P(col, row), P(col, row), P(row, col), P(col, row)),
        check_vma=False,
    )
```

```python
import jax
import jax.numpy as jnp
from jax import lax
from jax.experimental import pallas as pl
from jax.experimental.pallas import tpu as pltpu
from jax.sharding import Mesh, PartitionSpec as P

gelu_c = 0.7978845608
gelu_k = 0.044715
bf16 = jnp.bfloat16
f32 = jnp.float32

NZ, NX = 8, 4


def gelu_value(pre):
    inner = jnp.tanh(gelu_c * (pre + gelu_k * pre * pre * pre))
    return 0.5 * pre * (1.0 + inner)


def gelu_slope(pre):
    inner = jnp.tanh(gelu_c * (pre + gelu_k * pre * pre * pre))
    return 0.5 * (1.0 + inner) + 0.5 * pre * (1.0 - inner * inner) * gelu_c * (
        1.0 + 3.0 * gelu_k * pre * pre
    )


def dot_plain(left, right):
    return jnp.dot(left, right, preferred_element_type=f32)


def dot_last(left, right):
    return lax.dot_general(left, right, (((1,), (1,)), ((), ())), preferred_element_type=f32)


def dot_first(left, right):
    return lax.dot_general(left, right, (((0,), (0,)), ((), ())), preferred_element_type=f32)


def shift(a, axis, k, name=None):
    n = lax.axis_size(axis)
    with jax.named_scope(name or "move_" + axis):
        return lax.ppermute(a, axis, [(i, (i + k) % n) for i in range(n)])


def place_kernel(groups, table, mine, theirs, *outs):
    def take(s):
        at = lax.rem(s, 8)
        return jnp.where(s < 8, mine[at], theirs[at])

    n = mine.shape[1]
    for out, group in zip(outs, groups):
        for j, i in enumerate(group):
            out[j * n : (j + 1) * n] = take(table[i])
    outs[-1][0] = theirs[...]
    outs[-1][1] = mine[...]


def place(mine, theirs, groups, table):
    _, n, d = mine.shape
    vmem, smem = pl.BlockSpec(memory_space=pltpu.VMEM), pl.BlockSpec(memory_space=pltpu.SMEM)
    out = pl.pallas_call(
        lambda *refs: place_kernel(groups, *refs),
        out_shape=[jax.ShapeDtypeStruct((len(g) * n, d), bf16) for g in groups]
        + [jax.ShapeDtypeStruct((2, 8, n, d), bf16)],
        in_specs=[smem, vmem, vmem],
        out_specs=[vmem] * (len(groups) + 1),
        cost_estimate=pl.CostEstimate(flops=0, bytes_accessed=12 * mine.size, transcendentals=0),
        compiler_params=pltpu.CompilerParams(vmem_limit_bytes=8 << 20),
    )(table, mine, theirs)
    return out[:-1], out[-1]


def after_kernel(a, *rest):
    pass


def after(a, *earlier):
    any_ = pl.BlockSpec(memory_space=pl.ANY)
    return pl.pallas_call(
        after_kernel,
        out_shape=jax.ShapeDtypeStruct(a.shape, a.dtype),
        in_specs=[any_] * (1 + len(earlier)),
        out_specs=any_,
        input_output_aliases={0: 0},
        cost_estimate=pl.CostEstimate(flops=1, bytes_accessed=1, transcendentals=0),
        compiler_params=pltpu.CompilerParams(vmem_limit_bytes=1 << 17),
    )(a, *earlier)


def gather_x(pair, earlier=(), later=()):
    if earlier:
        pair = after(pair, *earlier)
    back = [shift(pair, "x", k) for k in (3, 2, 1)]
    if later:
        back[0] = after(back[0], *later)
    return jnp.concatenate([pair] + back)


def ring_z(own, first_up, name):
    got = [own] + [None] * 7
    n_up = 4 if first_up else 3
    for i in range(4):
        if i < n_up:
            got[7 - i] = shift(got[(8 - i) % 8], "z", 1, f"{name}{7 - i}")
        if i < 7 - n_up:
            got[1 + i] = shift(got[i], "z", -1, f"{name}{1 + i}")
    return got


def product_kernel(last, layout, table, *refs):
    blocks, w = refs[: len(layout)], refs[len(layout)]
    send, keep, whole = refs[1 + len(layout) :]
    _, _, n, ff = whole.shape
    z, flip, x, yh = table[16], table[17], table[18], table[19]
    for block, parts in zip(blocks, layout):
        for j, (far, k) in enumerate(parts):
            m = lax.rem(z + k, NZ)
            to = lax.rem(m // 2 - x + NX, NX) * 2 + jnp.abs(lax.rem(m, 2) - yh)
            whole[flip if far else 1 - flip, to] = block[j * n : (j + 1) * n]
    dims = (((1,), (1 if last else 0,)), ((), ()))

    @pl.loop(0, send.shape[-1] // 256)
    def _(j):
        at = pl.ds(pl.multiple_of(j * 256, 256), 256)
        right = w[at, :] if last else w[:, at]
        for i, out in enumerate((send, keep)):
            left = whole[i].reshape(NZ * n, ff)
            p = lax.dot_general(left, right, dims, preferred_element_type=f32)
            out[:, :, at] = p.reshape(NZ, n, 256)


def products(n, blocks, layout, w, last, table):
    ff = blocks[0].shape[1]
    d = w.shape[0] if last else w.shape[1]
    vmem = pl.BlockSpec(memory_space=pltpu.VMEM)
    return pl.pallas_call(
        lambda *refs: product_kernel(last, layout, *refs),
        out_shape=[jax.ShapeDtypeStruct((NZ, n, d), f32)] * 2
        + [jax.ShapeDtypeStruct((2, NZ, n, ff), bf16)],
        in_specs=[pl.BlockSpec(memory_space=pltpu.SMEM)] + [vmem] * (len(blocks) + 1),
        out_specs=[vmem] * 3,
        cost_estimate=pl.CostEstimate(
            flops=4 * NZ * n * ff * d, bytes_accessed=12 << 20, transcendentals=0
        ),
        compiler_params=pltpu.CompilerParams(vmem_limit_bytes=15 << 20),
    )(table, *blocks, w)


def send_x(keep, got, name):
    total, sent, back = keep[:2] + got[:2], [], []
    for rx in range(1, NX):
        sent.append((keep[2 * rx : 2 * rx + 2] + got[2 * rx : 2 * rx + 2]).astype(bf16))
        back.append(shift(sent[-1], "x", rx, f"{name}_x{rx}"))

    def sums(*earlier):
        first = after(back[0], *earlier) if earlier else back[0]
        return total + sum(b.astype(f32) for b in [first] + back[1:])

    return sent, sums


def step_kernel(last, starts, splits, a, w, *refs):
    got, outs = refs[: len(starts)], refs[len(refs) - len(splits) :]
    rows = a.shape[0]
    dims = (((1,), (1 if last else 0,)), ((), ()))

    tile = 256 if last else 768

    @pl.loop(0, outs[0].shape[1] // tile)
    def _(j):
        at = pl.ds(pl.multiple_of(j * tile, tile), tile)
        right = w[at, :] if last else w[:, at]
        p = lax.dot_general(a[...], right, dims, preferred_element_type=f32)
        for g, start in zip(got, starts):
            p = p + g[start : start + rows, at].astype(f32)
        for out, (first, end) in zip(outs, splits):
            out[:, at] = p[first:end].astype(out.dtype)


def step(a, w, last, got=(), outs=None, behind=()):
    rows, width = a.shape[0], w.shape[0] if last else w.shape[1]
    outs = outs or [(bf16, 0, rows)]
    vmem, any_ = pl.BlockSpec(memory_space=pltpu.VMEM), pl.BlockSpec(memory_space=pl.ANY)
    starts, splits = [g[1] for g in got], [o[1:] for o in outs]
    result = pl.pallas_call(
        lambda *refs: step_kernel(last, starts, splits, *refs),
        out_shape=[jax.ShapeDtypeStruct((end - first, width), t) for t, first, end in outs],
        in_specs=[vmem] * (2 + len(got)) + [any_] * len(behind),
        out_specs=[vmem] * len(outs),
        cost_estimate=pl.CostEstimate(
            flops=2 * rows * w.size, bytes_accessed=4 * rows * width, transcendentals=0
        ),
        compiler_params=pltpu.CompilerParams(vmem_limit_bytes=6 << 20),
    )(a, w, *[g[0] for g in got], *behind)
    return result if len(outs) > 1 else result[0]


def per_device(tokens, in_weight, out_weight, out_grad):
    z, yl = lax.axis_index("z"), lax.axis_index("yl")
    x, yh, c = lax.axis_index("x"), lax.axis_index("yh"), lax.axis_index("c")
    n, d = tokens.shape
    ff = in_weight.shape[1]
    i = jnp.arange(16, dtype=jnp.int32)
    to_z, to_yl = (z + i // 2) % NZ, yl ^ (i % 2)
    src = (to_yl ^ c) * 8 + (to_z // 2 - x) % NX * 2 + (to_z % 2 ^ yh)
    table = jnp.concatenate([src, jnp.stack([z, yl ^ c, x, yh]).astype(src.dtype)])

    def up(a, name="pieces"):
        return shift(a, "z", 1, name + "_up")

    def down(a, name="pieces"):
        return shift(a, "z", -1, name + "_down")

    def rows(a):
        return a.reshape(16 * n, a.shape[-1])

    other = shift(jnp.stack([tokens, out_grad]), "yh", 1, "both_yh")
    mine = gather_x(jnp.stack([tokens, other[0]]))
    pair_g = jnp.stack([out_grad, other[1]])
    tok, all_tok = place(
        mine, shift(mine, "c", 1), [(2 * k, 2 * k + 1) for k in range(NZ)], table
    )

    last_step = [mine]

    def chained(*given, **named):
        out = step(*given, behind=last_step[:], **named)
        last_step[:] = [out[0] if isinstance(out, (list, tuple)) else out]
        return out

    def pre_step(k, *got, **named):
        return chained(tok[k], in_weight, False, [(g, 0) for g in got], **named)

    def hid_step(k, *got, **named):
        return chained(grad[k], out_weight, True, [(g, 0) for g in got] + [from_y[k]], **named)

    def to_y(j, name):
        sent = chained(blocks[j], out_weight, True)
        got = shift(sent, "yl", 1, name)
        for i, k in enumerate(rounds[j]):
            from_y[k] = (got, i * n)

    from_y = {}
    rounds = ((4, 3), (5, 2), (6, 1), (7, 0))
    groups = [(2 * k,) for k in range(NZ)] + [tuple(2 * k + 1 for k in ks) for ks in rounds]

    p4 = pre_step(4)
    p_up = up(p4, "p4")
    p5 = pre_step(5)
    p_down = down(p5, "p5")
    p3 = pre_step(3, p_up)
    p_up = up(p3, "p3")
    p6 = pre_step(6, p_down)
    p_down = down(p6, "p6")

    mine_g = gather_x(pair_g, [mine], [p6])
    grad, all_grad = place(mine_g, shift(mine_g, "c", 1), groups, table)
    grad, blocks = grad[:NZ], grad[NZ:]

    to_y(0, "first_y")
    to_y(1, "second_y")
    p2 = pre_step(2, p_up)
    p_up = up(p2, "p2")
    p7 = pre_step(7, p_down)
    p_down = down(p7, "p7")
    p1 = pre_step(1, p_up)
    p_up = up(p1, "p1")
    h4 = hid_step(4)
    h_down = down(h4, "h4")
    to_y(2, "third_y")
    h3 = hid_step(3)
    h_up = up(h3, "h3")
    h5 = hid_step(5, h_down)
    h_down = down(h5, "h5")

    pre_near, pre_far = pre_step(0, p_up, p_down, outs=[(f32, 0, n), (bf16, n, 2 * n)])
    pre_got = shift(pre_far, "yl", 1, "pre_y")
    h2 = hid_step(2, h_up)
    h_up = up(h2, "h2")
    h6 = hid_step(6, h_down)
    h_down = down(h6, "h6")

    pre = pre_near + after(pre_got, h6).astype(f32)
    hidden = gelu_value(pre).astype(bf16)
    hidden_got = shift(hidden, "yl", 1, "hidden_y")
    last_step[:] = [hidden]
    to_y(3, "fourth_y")
    h1 = hid_step(1, h_up)
    h_up = up(h1, "h1")

    hid = ring_z(jnp.concatenate([hidden, hidden_got]), True, "hidden")

    h7 = hid_step(7, h_down)
    h_down = down(h7, "h7")
    last_step[:] = [hid[7], hid[1]]
    grad_sum = hid_step(0, h_up, h_down, outs=[(f32, 0, n)])
    pre_grad = (grad_sum * gelu_slope(pre)).astype(bf16)

    def to_pair(a, name, *earlier):
        return shift(after(a, *earlier) if earlier else a, "yl", 1, name)

    near = [pre_grad] + [None] * 7
    far0 = to_pair(pre_grad, "g0_y")
    near[7], near[1] = up(pre_grad, "g7"), down(pre_grad, "g1")
    far17 = to_pair(jnp.concatenate([near[1], near[7]]), "g17_y")
    near[6], near[2] = up(after(near[7], far0), "g6"), down(near[1], "g2")
    far26 = to_pair(jnp.concatenate([near[2], near[6]]), "g26_y")
    near[5], near[3] = up(after(near[6], far17), "g5"), down(near[2], "g3")
    far35 = to_pair(jnp.concatenate([near[3], near[5]]), "g35_y")
    near[4] = up(after(near[5], far26), "g4")
    far4 = to_pair(near[4], "g4_y")

    pairs = [((0, k), (1, k)) for k in range(NZ)]
    send, keep, all_hidden = products(
        n, hid, pairs, out_weight, False, after(table, far35, near[4])
    )
    out_sent, out_sums = send_x(keep, shift(send, "c", 1, "out_core"), "out")

    layout = [((0, k),) for k in range(NZ)]
    layout += [tuple((1, k) for k in ks) for ks in ((0,), (1, 7), (2, 6), (3, 5), (4,))]
    send, keep, all_pre_grad = products(
        n, near + [far0, far17, far26, far35, far4], layout, in_weight, True, after(table, *out_sent)
    )
    first_grad = dot_first(rows(all_tok), rows(all_pre_grad)).astype(bf16)
    total = out_sums()
    out_near, out_far = total[0], total[1].astype(bf16)

    got = after(shift(send, "c", 1, "token_core"), first_grad, out_far)
    sent, sums = send_x(keep, got, "token")
    second_grad = dot_first(rows(all_hidden), rows(after(all_grad, *sent))).astype(bf16)
    total = sums(second_grad)
    token_grad = (total[0] + shift(total[1], "yh", 1, "token_yh")).astype(bf16)
    out_got = shift(after(out_far, *sent), "yh", 1, "out_yh")
    layer_out = (out_near + out_got.astype(f32)).astype(bf16)
    return (layer_out, token_grad, first_grad, second_grad)


def solution(mesh):
    fine = Mesh(mesh.devices.reshape(8, 2, 4, 2, 2), ("z", "yl", "x", "yh", "c"))
    row, col = ("z", "yl"), ("x", "yh", "c")
    return jax.shard_map(
        per_device,
        mesh=fine,
        in_specs=(P(col, row), P(row, col), P(col, row), P(col, row)),
        out_specs=(P(col, row), P(col, row), P(row, col), P(col, row)),
        check_vma=False,
    )
```

```python
import jax
import jax.numpy as jnp
from jax import lax
from jax.experimental import pallas as pl
from jax.experimental.pallas import tpu as pltpu
from jax.sharding import Mesh, PartitionSpec as P

gelu_c = 0.7978845608
gelu_k = 0.044715
bf16 = jnp.bfloat16
f32 = jnp.float32

NZ, NX = 8, 4


def gelu_value(pre):
    inner = jnp.tanh(gelu_c * (pre + gelu_k * pre * pre * pre))
    return 0.5 * pre * (1.0 + inner)


def gelu_slope(pre):
    inner = jnp.tanh(gelu_c * (pre + gelu_k * pre * pre * pre))
    return 0.5 * (1.0 + inner) + 0.5 * pre * (1.0 - inner * inner) * gelu_c * (
        1.0 + 3.0 * gelu_k * pre * pre
    )


def dot_plain(left, right):
    return jnp.dot(left, right, preferred_element_type=f32)


def dot_last(left, right):
    return lax.dot_general(left, right, (((1,), (1,)), ((), ())), preferred_element_type=f32)


def dot_first(left, right):
    return lax.dot_general(left, right, (((0,), (0,)), ((), ())), preferred_element_type=f32)


def shift(a, axis, k, name=None):
    n = lax.axis_size(axis)
    with jax.named_scope(name or "move_" + axis):
        return lax.ppermute(a, axis, [(i, (i + k) % n) for i in range(n)])


def place_kernel(groups, table, mine, theirs, *outs):
    def take(s):
        at = lax.rem(s, 8)
        return jnp.where(s < 8, mine[at], theirs[at])

    n = mine.shape[1]
    for out, group in zip(outs, groups):
        for j, i in enumerate(group):
            out[j * n : (j + 1) * n] = take(table[i])
    outs[-1][0] = theirs[...]
    outs[-1][1] = mine[...]


def place(mine, theirs, groups, table):
    _, n, d = mine.shape
    vmem, smem = pl.BlockSpec(memory_space=pltpu.VMEM), pl.BlockSpec(memory_space=pltpu.SMEM)
    out = pl.pallas_call(
        lambda *refs: place_kernel(groups, *refs),
        out_shape=[jax.ShapeDtypeStruct((len(g) * n, d), bf16) for g in groups]
        + [jax.ShapeDtypeStruct((2, 8, n, d), bf16)],
        in_specs=[smem, vmem, vmem],
        out_specs=[vmem] * (len(groups) + 1),
        cost_estimate=pl.CostEstimate(flops=0, bytes_accessed=12 * mine.size, transcendentals=0),
        compiler_params=pltpu.CompilerParams(vmem_limit_bytes=8 << 20),
    )(table, mine, theirs)
    return out[:-1], out[-1]


def after_kernel(a, *rest):
    pass


def after(a, *earlier):
    any_ = pl.BlockSpec(memory_space=pl.ANY)
    return pl.pallas_call(
        after_kernel,
        out_shape=jax.ShapeDtypeStruct(a.shape, a.dtype),
        in_specs=[any_] * (1 + len(earlier)),
        out_specs=any_,
        input_output_aliases={0: 0},
        cost_estimate=pl.CostEstimate(flops=1, bytes_accessed=1, transcendentals=0),
        compiler_params=pltpu.CompilerParams(vmem_limit_bytes=1 << 17),
    )(a, *earlier)


def gather_x(pair, earlier=(), later=()):
    if earlier:
        pair = after(pair, *earlier)
    back = [shift(pair, "x", k) for k in (3, 2, 1)]
    if later:
        back[0] = after(back[0], *later)
    return jnp.concatenate([pair] + back)


def ring_z(own, first_up, name):
    got = [own] + [None] * 7
    n_up = 4 if first_up else 3
    for i in range(4):
        if i < n_up:
            got[7 - i] = shift(got[(8 - i) % 8], "z", 1, f"{name}{7 - i}")
        if i < 7 - n_up:
            got[1 + i] = shift(got[i], "z", -1, f"{name}{1 + i}")
    return got


def product_kernel(last, layout, table, *refs):
    blocks, w = refs[: len(layout)], refs[len(layout)]
    send, keep, whole = refs[1 + len(layout) :]
    _, _, n, ff = whole.shape
    z, flip, x, yh = table[16], table[17], table[18], table[19]
    for block, parts in zip(blocks, layout):
        for j, (far, k) in enumerate(parts):
            m = lax.rem(z + k, NZ)
            to = lax.rem(m // 2 - x + NX, NX) * 2 + jnp.abs(lax.rem(m, 2) - yh)
            whole[flip if far else 1 - flip, to] = block[j * n : (j + 1) * n]
    dims = (((1,), (1 if last else 0,)), ((), ()))

    @pl.loop(0, send.shape[-1] // 256)
    def _(j):
        at = pl.ds(pl.multiple_of(j * 256, 256), 256)
        right = w[at, :] if last else w[:, at]
        for i, out in enumerate((send, keep)):
            left = whole[i].reshape(NZ * n, ff)
            p = lax.dot_general(left, right, dims, preferred_element_type=f32)
            out[:, :, at] = p.reshape(NZ, n, 256)


def products(n, blocks, layout, w, last, table):
    ff = blocks[0].shape[1]
    d = w.shape[0] if last else w.shape[1]
    vmem = pl.BlockSpec(memory_space=pltpu.VMEM)
    return pl.pallas_call(
        lambda *refs: product_kernel(last, layout, *refs),
        out_shape=[jax.ShapeDtypeStruct((NZ, n, d), f32)] * 2
        + [jax.ShapeDtypeStruct((2, NZ, n, ff), bf16)],
        in_specs=[pl.BlockSpec(memory_space=pltpu.SMEM)] + [vmem] * (len(blocks) + 1),
        out_specs=[vmem] * 3,
        cost_estimate=pl.CostEstimate(
            flops=4 * NZ * n * ff * d, bytes_accessed=12 << 20, transcendentals=0
        ),
        compiler_params=pltpu.CompilerParams(vmem_limit_bytes=15 << 20),
    )(table, *blocks, w)


def send_x(keep, got, name):
    total, sent, back = keep[:2] + got[:2], [], []
    for rx in range(1, NX):
        sent.append((keep[2 * rx : 2 * rx + 2] + got[2 * rx : 2 * rx + 2]).astype(bf16))
        back.append(shift(sent[-1], "x", rx, f"{name}_x{rx}"))

    def sums(*earlier):
        first = after(back[0], *earlier) if earlier else back[0]
        return total + sum(b.astype(f32) for b in [first] + back[1:])

    return sent, sums


def step_kernel(last, starts, splits, a, w, *refs):
    got, outs = refs[: len(starts)], refs[len(refs) - len(splits) :]
    rows = a.shape[0]
    dims = (((1,), (1 if last else 0,)), ((), ()))

    tile = 384 if last else 768

    @pl.loop(0, outs[0].shape[1] // tile)
    def _(j):
        at = pl.ds(pl.multiple_of(j * tile, tile), tile)
        right = w[at, :] if last else w[:, at]
        p = lax.dot_general(a[...], right, dims, preferred_element_type=f32)
        for g, start in zip(got, starts):
            p = p + g[start : start + rows, at].astype(f32)
        for out, (first, end) in zip(outs, splits):
            out[:, at] = p[first:end].astype(out.dtype)


def step(a, w, last, got=(), outs=None, behind=()):
    rows, width = a.shape[0], w.shape[0] if last else w.shape[1]
    outs = outs or [(bf16, 0, rows)]
    vmem, any_ = pl.BlockSpec(memory_space=pltpu.VMEM), pl.BlockSpec(memory_space=pl.ANY)
    starts, splits = [g[1] for g in got], [o[1:] for o in outs]
    result = pl.pallas_call(
        lambda *refs: step_kernel(last, starts, splits, *refs),
        out_shape=[jax.ShapeDtypeStruct((end - first, width), t) for t, first, end in outs],
        in_specs=[vmem] * (2 + len(got)) + [any_] * len(behind),
        out_specs=[vmem] * len(outs),
        cost_estimate=pl.CostEstimate(
            flops=2 * rows * w.size, bytes_accessed=4 * rows * width, transcendentals=0
        ),
        compiler_params=pltpu.CompilerParams(vmem_limit_bytes=6 << 20),
    )(a, w, *[g[0] for g in got], *behind)
    return result if len(outs) > 1 else result[0]


def per_device(tokens, in_weight, out_weight, out_grad):
    z, yl = lax.axis_index("z"), lax.axis_index("yl")
    x, yh, c = lax.axis_index("x"), lax.axis_index("yh"), lax.axis_index("c")
    n, d = tokens.shape
    ff = in_weight.shape[1]
    i = jnp.arange(16, dtype=jnp.int32)
    to_z, to_yl = (z + i // 2) % NZ, yl ^ (i % 2)
    src = (to_yl ^ c) * 8 + (to_z // 2 - x) % NX * 2 + (to_z % 2 ^ yh)
    table = jnp.concatenate([src, jnp.stack([z, yl ^ c, x, yh]).astype(src.dtype)])

    def up(a, name="pieces"):
        return shift(a, "z", 1, name + "_up")

    def down(a, name="pieces"):
        return shift(a, "z", -1, name + "_down")

    def rows(a):
        return a.reshape(16 * n, a.shape[-1])

    other, other_g = shift(tokens, "yh", 1, "tokens_yh"), shift(out_grad, "yh", 1, "grads_yh")
    mine = gather_x(jnp.stack([tokens, other]), [other_g])
    pair_g = jnp.stack([out_grad, other_g])
    tok, all_tok = place(
        mine, shift(mine, "c", 1), [(2 * k, 2 * k + 1) for k in range(NZ)], table
    )

    last_step = [mine]

    def chained(*given, **named):
        out = step(*given, behind=last_step[:], **named)
        last_step[:] = [out[0] if isinstance(out, (list, tuple)) else out]
        return out

    def pre_step(k, *got, **named):
        return chained(tok[k], in_weight, False, [(g, 0) for g in got], **named)

    def hid_step(k, *got, **named):
        return chained(grad[k], out_weight, True, [(g, 0) for g in got] + [from_y[k]], **named)

    def to_y(j, name):
        sent = chained(blocks[j], out_weight, True)
        got = shift(sent, "yl", 1, name)
        for i, k in enumerate(rounds[j]):
            from_y[k] = (got, i * n)

    from_y = {}
    rounds = ((4, 3), (5, 2), (6, 1), (7, 0))
    groups = [(2 * k,) for k in range(NZ)] + [tuple(2 * k + 1 for k in ks) for ks in rounds]

    p4 = pre_step(4)
    p_up = up(p4, "p4")
    p5 = pre_step(5)
    p_down = down(p5, "p5")
    p3 = pre_step(3, p_up)
    p_up = up(p3, "p3")
    p6 = pre_step(6, p_down)
    p_down = down(p6, "p6")

    mine_g = gather_x(pair_g, [mine], [p6])
    grad, all_grad = place(mine_g, shift(mine_g, "c", 1), groups, table)
    grad, blocks = grad[:NZ], grad[NZ:]

    to_y(0, "first_y")
    to_y(1, "second_y")
    p2 = pre_step(2, p_up)
    p_up = up(p2, "p2")
    p7 = pre_step(7, p_down)
    p_down = down(p7, "p7")
    p1 = pre_step(1, p_up)
    p_up = up(p1, "p1")
    h4 = hid_step(4)
    h_down = down(h4, "h4")
    to_y(2, "third_y")
    h3 = hid_step(3)
    h_up = up(h3, "h3")
    h5 = hid_step(5, h_down)
    h_down = down(h5, "h5")

    pre_near, pre_far = pre_step(0, p_up, p_down, outs=[(f32, 0, n), (bf16, n, 2 * n)])
    pre_got = shift(pre_far, "yl", 1, "pre_y")
    h2 = hid_step(2, h_up)
    h_up = up(h2, "h2")
    h6 = hid_step(6, h_down)
    h_down = down(h6, "h6")

    pre = pre_near + after(pre_got, h6).astype(f32)
    hidden = gelu_value(pre).astype(bf16)
    hidden_got = shift(hidden, "yl", 1, "hidden_y")
    last_step[:] = [hidden]
    to_y(3, "fourth_y")
    h1 = hid_step(1, h_up)
    h_up = up(h1, "h1")

    hid = ring_z(jnp.concatenate([hidden, hidden_got]), True, "hidden")

    h7 = hid_step(7, h_down)
    h_down = down(h7, "h7")
    last_step[:] = [hid[7], hid[1]]
    grad_sum = hid_step(0, h_up, h_down, outs=[(f32, 0, n)])
    pre_grad = (grad_sum * gelu_slope(pre)).astype(bf16)

    def to_pair(a, name, *earlier):
        return shift(after(a, *earlier) if earlier else a, "yl", 1, name)

    near = [pre_grad] + [None] * 7
    far0 = to_pair(pre_grad, "g0_y")
    near[7], near[1] = up(pre_grad, "g7"), down(pre_grad, "g1")
    far17 = to_pair(jnp.concatenate([near[1], near[7]]), "g17_y")
    near[6], near[2] = up(after(near[7], far0), "g6"), down(near[1], "g2")
    far26 = to_pair(jnp.concatenate([near[2], near[6]]), "g26_y")
    near[5], near[3] = up(after(near[6], far17), "g5"), down(near[2], "g3")
    far35 = to_pair(jnp.concatenate([near[3], near[5]]), "g35_y")
    near[4] = up(after(near[5], far26), "g4")
    far4 = to_pair(near[4], "g4_y")

    pairs = [((0, k), (1, k)) for k in range(NZ)]
    send, keep, all_hidden = products(
        n, hid, pairs, out_weight, False, after(table, far35, near[4])
    )
    out_sent, out_sums = send_x(keep, shift(send, "c", 1, "out_core"), "out")

    layout = [((0, k),) for k in range(NZ)]
    layout += [tuple((1, k) for k in ks) for ks in ((0,), (1, 7), (2, 6), (3, 5), (4,))]
    send, keep, all_pre_grad = products(
        n, near + [far0, far17, far26, far35, far4], layout, in_weight, True, after(table, *out_sent)
    )
    first_grad = dot_first(rows(all_tok), rows(all_pre_grad)).astype(bf16)
    total = out_sums()
    out_near, out_far = total[0], total[1].astype(bf16)

    got = after(shift(send, "c", 1, "token_core"), first_grad, out_far)
    sent, sums = send_x(keep, got, "token")
    second_grad = dot_first(rows(all_hidden), rows(after(all_grad, *sent))).astype(bf16)
    total = sums(second_grad)
    token_grad = (total[0] + shift(total[1], "yh", 1, "token_yh")).astype(bf16)
    out_got = shift(after(out_far, *sent), "yh", 1, "out_yh")
    layer_out = (out_near + out_got.astype(f32)).astype(bf16)
    return (layer_out, token_grad, first_grad, second_grad)


def solution(mesh):
    fine = Mesh(mesh.devices.reshape(8, 2, 4, 2, 2), ("z", "yl", "x", "yh", "c"))
    row, col = ("z", "yl"), ("x", "yh", "c")
    return jax.shard_map(
        per_device,
        mesh=fine,
        in_specs=(P(col, row), P(row, col), P(col, row), P(col, row)),
        out_specs=(P(col, row), P(col, row), P(row, col), P(col, row)),
        check_vma=False,
    )
```
